256 devices in a mesh: dp: 2 (over x_hi), mp: 128 (over y, x_lo, z, core).
Axes of the slice: x: 4 (x_hi: 2, x_lo: 2; x = x_hi * 2 + x_lo), y: 4, z: 8, core: 2. Of those that a mesh axis runs over, the one named last changes fastest.
Arguments:
- activations: bfloat16 [2048, 16384], P('dp', 'mp'), may hold values from -6 to 6
- left_up: bfloat16 [128, 128, 128], P('mp'), may hold values from -0.5 to 0.5
- right_up: bfloat16 [128, 128, 128], P('mp'), may hold values from -0.5 to 0.5
- left_down: bfloat16 [128, 128, 128], P('mp'), may hold values from -0.5 to 0.5
- right_down: bfloat16 [128, 128, 128], P('mp'), may hold values from -0.5 to 0.5
- cotangent: bfloat16 [2048, 16384], P('dp', 'mp'), may hold values from -6 to 6
Outputs:
- mlp_output: bfloat16 [2048, 16384], P('dp', 'mp')
- input_grad: bfloat16 [2048, 16384], P('dp', 'mp')
- leftup_grad: float32 [128, 128, 128], P('mp')
- rightup_grad: float32 [128, 128, 128], P('mp')
- leftdown_grad: float32 [128, 128, 128], P('mp')
- rightdown_grad: float32 [128, 128, 128], P('mp')
The draws below stay inside these ranges and needn't reach their ends.
All inputs are finite; a program needn't handle non-finite values.
Results may differ from the reference program's by a relative error of at most 0.011.
Values may be sent and summed in bfloat16 or wider, within the bound.
No kernel may reach another device: no remote copies, remote signals or barrier semaphores. Data moves between devices by JAX's collectives and lax.ppermute only.
A program may use at most 64 MiB of HBM per device.

```python
import math
import jax
import jax.numpy as jnp
from jax import lax

NB = 128
BS = 128
WIDTH = 16384
TOKENS = 2048


def steps_of(own_key, extent, shards, smallest, largest):
    loudness, own = 1.0, jax.random.fold_in(own_key, 6)
    for position, blocks in shards:
        heights = jnp.exp(jax.random.uniform(jax.random.fold_in(own, position), (blocks,), jnp.float32, smallest / len(shards), largest / len(shards)))
        loudness = loudness * jnp.repeat(heights, extent[position] // blocks).reshape([-1 if axis == position else 1 for axis in range(len(extent))])
    return loudness


def bell_draw(key, shape, width, most, pieces=(), dtype=jnp.bfloat16):
    level = steps_of(key, shape, pieces, -0.22, 0.18) if pieces else 1.0
    result = jax.random.normal(key, shape, jnp.float32) * width * level
    return jnp.minimum(jnp.maximum(result, -most), most).astype(dtype)


def setup_inputs(seed: int = 0) -> dict:
    keys = jax.random.split(jax.random.key(seed), 7)
    return {
        "activations": bell_draw(keys[0], (TOKENS, WIDTH), 1.0, 6.0, ((0, 2), (1, 128))),
        "left_up": bell_draw(keys[1], (NB, BS, BS), BS ** -0.5, 0.5, ((0, 128),)),
        "right_up": bell_draw(keys[2], (BS, NB, BS), NB ** -0.5, 0.5, ((0, 128),)),
        "left_down": bell_draw(keys[3], (NB, BS, BS), BS ** -0.5, 0.5, ((0, 128),)),
        "right_down": bell_draw(keys[4], (BS, NB, BS), NB ** -0.5, 0.5, ((0, 128),)),
        "cotangent": bell_draw(keys[5], (TOKENS, WIDTH), 1.0, 6.0, ((0, 2), (1, 128))),
    }


def gelu_exact(value):
    return 0.5 * value * (1.0 + lax.erf(value / math.sqrt(2.0)))

def gelu_slope(value):
    cumul = 0.5 * (1.0 + lax.erf(value / math.sqrt(2.0)))
    density = jnp.exp(-0.5 * value * value) / math.sqrt(2.0 * math.pi)
    return cumul + value * density

def block_left(vector, factor):
    count = vector.shape[0]
    shaped = vector.reshape(count, NB, BS).astype(jnp.float32)
    return jnp.einsum('tbi,bij->tbj', shaped, factor.astype(jnp.float32)).astype(jnp.bfloat16)

def block_right(blocks, factor):
    return jnp.einsum('tbj,jbk->tjk', blocks.astype(jnp.float32), factor.astype(jnp.float32))

def reference(activations, left_up, right_up, left_down, right_down, cotangent):
    block = math.gcd(TOKENS, 2048)
    steps_count = TOKENS // block
    acts = activations.reshape(steps_count, block, WIDTH)
    cots = cotangent.reshape(steps_count, block, WIDTH)
    lu = left_up.astype(jnp.float32)
    ru = right_up.astype(jnp.float32)
    ld = left_down.astype(jnp.float32)
    rd = right_down.astype(jnp.float32)

    def one_block(carry, pair):
        grad_lu, grad_ru, grad_ld, grad_rd = carry
        xblock, gblock = pair
        first_blk = block_left(xblock, left_up)
        pre_act = block_right(first_blk, right_up)
        hidden = gelu_exact(pre_act).astype(jnp.bfloat16)
        second_blk = block_left(hidden.reshape(block, WIDTH), left_down)
        output = block_right(second_blk, right_down).astype(jnp.bfloat16).reshape(block, WIDTH)
        gview = gblock.reshape(block, BS, BS).astype(jnp.float32)
        grad_rd = grad_rd + jnp.einsum('tbj,tjk->jbk', second_blk.astype(jnp.float32), gview)
        second_back = jnp.einsum('tjk,jbk->tbj', gview, rd).astype(jnp.bfloat16)
        hview = hidden.reshape(block, NB, BS).astype(jnp.float32)
        grad_ld = grad_ld + jnp.einsum('tbi,tbj->bij', hview, second_back.astype(jnp.float32))
        hidden_back = jnp.einsum('tbj,bij->tbi', second_back.astype(jnp.float32), ld)
        pre_back = (hidden_back * gelu_slope(pre_act)).astype(jnp.bfloat16).astype(jnp.float32)
        grad_ru = grad_ru + jnp.einsum('tbj,tjk->jbk', first_blk.astype(jnp.float32), pre_back)
        first_back = jnp.einsum('tjk,jbk->tbj', pre_back, ru).astype(jnp.bfloat16).astype(jnp.float32)
        xview = xblock.reshape(block, NB, BS).astype(jnp.float32)
        grad_lu = grad_lu + jnp.einsum('tbi,tbj->bij', xview, first_back)
        input_back = jnp.einsum('tbj,bij->tbi', first_back, lu).astype(jnp.bfloat16).reshape(block, WIDTH)
        return ((grad_lu, grad_ru, grad_ld, grad_rd), (output, input_back))
    zeros_left = jnp.zeros((NB, BS, BS), jnp.float32)
    zeros_right = jnp.zeros((BS, NB, BS), jnp.float32)
    grads, outs = lax.scan(one_block, (zeros_left, zeros_right, zeros_left, zeros_right), (acts, cots))
    mlp_output = outs[0].reshape(TOKENS, WIDTH)
    input_grad = outs[1].reshape(TOKENS, WIDTH)
    return (mlp_output, input_grad, grads[0], grads[1], grads[2], grads[3])
```

```python
import math

import jax
import jax.numpy as jnp
from jax import lax
from jax.experimental import pallas as pl
from jax.experimental.pallas import tpu as pltpu
from jax.sharding import PartitionSpec as P

F32 = jnp.float32
BF16 = jnp.bfloat16
LANES = 128


def gelu_exact(value):
    return 0.5 * value * (1.0 + lax.erf(value / math.sqrt(2.0)))


def gelu_slope(value):
    cumul = 0.5 * (1.0 + lax.erf(value / math.sqrt(2.0)))
    density = jnp.exp(-0.5 * value * value) / math.sqrt(2.0 * math.pi)
    return cumul + value * density


def dot(a, b, ca, cb):
    return lax.dot_general(a, b, (((ca,), (cb,)), ((), ())), preferred_element_type=F32)


def pack(flat):
    return flat.reshape(flat.shape[0], flat.shape[1] // LANES, LANES).astype(BF16)


def unpack(pieces):
    return pieces.astype(F32).reshape(pieces.shape[0], pieces.shape[1] * LANES).astype(BF16)


def send_kernel(x_ref, g_ref, lu_ref, rd_ref, out_ref):
    half = out_ref.shape[1] // 2
    out_ref[:, :half, :] = pack(dot(lu_ref[...], x_ref[...], 0, 1))
    out_ref[:, half:, :] = pack(dot(rd_ref[...], g_ref[...], 1, 1))


def middle_kernel(recv_ref, ru_ref, ld_ref, out_ref, hid_ref, pre_ref):
    half = recv_ref.shape[1] // 2
    ru, ld = ru_ref[...], ld_ref[...]
    pre_act = dot(ru, unpack(recv_ref[:, :half, :]), 0, 0)
    hidden = gelu_exact(pre_act).astype(BF16)
    hid_ref[...] = hidden
    out_ref[:, :half, :] = pack(dot(ld, hidden, 0, 0))
    hidden_back = dot(ld, unpack(recv_ref[:, half:, :]), 1, 0)
    pre_back = (hidden_back * gelu_slope(pre_act)).astype(BF16)
    pre_ref[...] = pre_back
    out_ref[:, half:, :] = pack(dot(ru, pre_back, 1, 0))


def middle_grads_kernel(recv_ref, hid_ref, pre_ref, grads_ref):
    half = recv_ref.shape[1] // 2
    grads_ref[0] = dot(unpack(recv_ref[:, :half, :]), pre_ref[...], 1, 1).astype(BF16)
    grads_ref[1] = dot(hid_ref[...], unpack(recv_ref[:, half:, :]), 1, 1).astype(BF16)


def last_grads_kernel(recv_ref, x_ref, g_ref, grads_ref):
    half = recv_ref.shape[1] // 2
    grads_ref[0] = dot(unpack(recv_ref[:, :half, :]), g_ref[...], 1, 0).astype(BF16)
    grads_ref[1] = dot(unpack(recv_ref[:, half:, :]), x_ref[...], 1, 0).T.astype(BF16)


def last_kernel(recv_ref, lu_ref, rd_ref, out_ref, back_ref):
    half = recv_ref.shape[1] // 2
    out_ref[...] = dot(unpack(recv_ref[:, :half, :]), rd_ref[...], 0, 0).astype(BF16)
    back_ref[...] = dot(unpack(recv_ref[:, half:, :]), lu_ref[...], 0, 1).astype(BF16)


def call(kernel, outs, flops, *args):
    moved = sum(a.size * 2 for a in args) + sum(math.prod(o) * 2 for o in outs)
    single = len(outs) == 1
    shapes = [jax.ShapeDtypeStruct(o, BF16) for o in outs]
    return pl.pallas_call(
        kernel,
        out_shape=shapes[0] if single else shapes,
        compiler_params=pltpu.CompilerParams(vmem_limit_bytes=48 * 1024 * 1024),
        cost_estimate=pl.CostEstimate(flops=flops, bytes_accessed=moved, transcendentals=0),
    )(*args)


def exchange(pieces):
    return lax.all_to_all(pieces, "mp", split_axis=0, concat_axis=0, tiled=True)


def body(activations, left_up, right_up, left_down, right_down, cotangent):
    count, order = activations.shape
    lu, ru, ld, rd = (w.reshape(w.shape[1:]) for w in (left_up, right_up, left_down, right_down))
    message = (order, 2 * count // LANES, LANES)
    unit = 2 * count * order * order
    pair = [(0, 1), (1, 0)]

    sent = call(send_kernel, [message], 2 * unit, activations, cotangent, lu, rd)
    first = exchange(sent)
    sent, hidden, pre_back = call(
        middle_kernel, [message, (order, count), (order, count)], 4 * unit, first, ru, ld
    )
    second = exchange(sent)
    mid = call(middle_grads_kernel, [(2, order, order)], 2 * unit, first, hidden, pre_back)
    mid_other = lax.ppermute(mid, "dp", pair)
    last = call(last_grads_kernel, [(2, order, order)], 2 * unit, second, activations, cotangent)
    last_other = lax.ppermute(last, "dp", pair)
    output, input_grad = call(
        last_kernel, [(count, order), (count, order)], 2 * unit, second, lu, rd
    )
    mid_sum = mid.astype(F32) + mid_other.astype(F32)
    last_sum = last.astype(F32) + last_other.astype(F32)
    return (output, input_grad, last_sum[1:], mid_sum[:1], mid_sum[1:], last_sum[:1])


def solution(mesh):
    tokens, factor = P("dp", "mp"), P("mp", None, None)
    return jax.shard_map(
        body,
        mesh=mesh,
        in_specs=(tokens, factor, factor, factor, factor, tokens),
        out_specs=(tokens, tokens, factor, factor, factor, factor),
        check_vma=False,
    )
```

```python
import functools
import math

import jax
import jax.numpy as jnp
import numpy as np
from jax import lax
from jax.experimental import pallas as pl
from jax.experimental.pallas import tpu as pltpu
from jax.sharding import PartitionSpec as P

F32 = jnp.float32
BF16 = jnp.bfloat16
LANES = 128
MP_AXES = (4, 2, 8, 2)
PART_VMEM, WHOLE_VMEM = 48 * 1024 * 1024, 60 * 1024 * 1024
IN_HBM = pl.BlockSpec(memory_space=pltpu.HBM)
IN_VMEM = pl.BlockSpec(memory_space=pltpu.VMEM)


def gelu_exact(value):
    return 0.5 * value * (1.0 + lax.erf(value / math.sqrt(2.0)))


def gelu_slope(value):
    cumul = 0.5 * (1.0 + lax.erf(value / math.sqrt(2.0)))
    density = jnp.exp(-0.5 * value * value) / math.sqrt(2.0 * math.pi)
    return cumul + value * density


def dot(a, b, ca, cb):
    return lax.dot_general(a, b, (((ca,), (cb,)), ((), ())), preferred_element_type=F32)


def runs_of(order):
    runs = []
    for position, member in enumerate(order):
        if runs and member == runs[-1][1] + runs[-1][2]:
            runs[-1][2] += 1
        else:
            runs.append([position, member, 1])
    return sorted((tuple(run) for run in runs), key=lambda run: run[1])


def put(ref, half, runs, flat):
    rows = ref.shape[1] // 2
    pieces = flat.astype(BF16).reshape(flat.shape[0], rows, LANES)
    for position, member, length in runs:
        ref[pl.ds(position, length), pl.ds(half * rows, rows), :] = pieces[member : member + length]


def take(ref, half, runs):
    rows = ref.shape[1] // 2
    pieces = [ref[pl.ds(p, length), pl.ds(half * rows, rows), :] for p, _, length in runs]
    pieces = pieces[0] if len(pieces) == 1 else jnp.concatenate(pieces, axis=0)
    return pieces.reshape(pieces.shape[0], rows * LANES)


def ship(half, out_ref, out_hbm, sems):
    rows = out_ref.shape[1] // 2
    part = pl.ds(half * rows, rows)
    return pltpu.make_async_copy(out_ref.at[:, part, :], out_hbm.at[:, part, :], sems.at[half])


def send_kernel(
    runs, x_hbm, g_hbm, lu_hbm, rd_hbm, out_hbm, x_ref, g_ref, lu_ref, rd_ref, out_ref, in_sems, sems
):
    pairs = ((lu_hbm, lu_ref), (x_hbm, x_ref), (rd_hbm, rd_ref), (g_hbm, g_ref))
    copies = [pltpu.make_async_copy(a, b, in_sems.at[i]) for i, (a, b) in enumerate(pairs)]
    for copy in copies:
        copy.start()
    copies[0].wait()
    copies[1].wait()
    put(out_ref, 0, runs, dot(lu_ref[...], x_ref[...], 0, 1))
    first = ship(0, out_ref, out_hbm, sems)
    first.start()
    copies[2].wait()
    copies[3].wait()
    put(out_ref, 1, runs, dot(rd_ref[...], g_ref[...], 1, 1))
    second = ship(1, out_ref, out_hbm, sems)
    second.start()
    first.wait()
    second.wait()


def middle_kernel(came, runs, recv_ref, ru_ref, ld_ref, out_hbm, hid_ref, pre_ref, out_ref, sems):
    ru, ld = ru_ref[...], ld_ref[...]
    pre_act = dot(ru, take(recv_ref, 0, came), 0, 0)
    hidden = gelu_exact(pre_act).astype(BF16)
    put(out_ref, 0, runs, dot(ld, hidden, 0, 0))
    first = ship(0, out_ref, out_hbm, sems)
    first.start()
    hid_ref[...] = hidden
    hidden_back = dot(ld, take(recv_ref, 1, came), 1, 0)
    pre_back = (hidden_back * gelu_slope(pre_act)).astype(BF16)
    put(out_ref, 1, runs, dot(ru, pre_back, 1, 0))
    second = ship(1, out_ref, out_hbm, sems)
    second.start()
    pre_ref[...] = pre_back
    first.wait()
    second.wait()


def middle_grads_kernel(came, recv_ref, hid_ref, pre_ref, grads_ref):
    grads_ref[0] = dot(take(recv_ref, 0, came), pre_ref[...], 1, 1).astype(BF16)
    grads_ref[1] = dot(hid_ref[...], take(recv_ref, 1, came), 1, 1).astype(BF16)


def last_grads_kernel(came, recv_ref, x_ref, g_ref, grads_ref):
    grads_ref[0] = dot(take(recv_ref, 0, came), g_ref[...], 1, 0).astype(BF16)
    grads_ref[1] = dot(take(recv_ref, 1, came), x_ref[...], 1, 0).T.astype(BF16)


def last_kernel(came, recv_ref, lu_ref, rd_ref, out_ref, back_ref):
    out_ref[...] = dot(take(recv_ref, 0, came), rd_ref[...], 0, 0).astype(BF16)
    back_ref[...] = dot(take(recv_ref, 1, came), lu_ref[...], 0, 1).astype(BF16)


def call(kernel, outs, flops, *args, scratch=(), vmem=PART_VMEM, **specs):
    moved = sum(a.size * 2 for a in args) + sum(math.prod(o) * 2 for o in outs)
    single = len(outs) == 1
    shapes = [jax.ShapeDtypeStruct(o, BF16) for o in outs]
    return pl.pallas_call(
        kernel,
        out_shape=shapes[0] if single else shapes,
        scratch_shapes=list(scratch),
        compiler_params=pltpu.CompilerParams(vmem_limit_bytes=vmem),
        cost_estimate=pl.CostEstimate(flops=flops, bytes_accessed=moved, transcendentals=0),
        **specs,
    )(*args)


def exchange(pieces, order):
    return lax.all_to_all(
        pieces, "mp", split_axis=0, concat_axis=0, tiled=True, axis_index_groups=[list(order)]
    )


def body(order, activations, left_up, right_up, left_down, right_down, cotangent):
    count, size = activations.shape
    lu, ru, ld, rd = (w.reshape(w.shape[1:]) for w in (left_up, right_up, left_down, right_down))
    message = (size, 2 * count // LANES, LANES)
    square, wide, tall = (size, size), (size, count), (count, size)
    unit = 2 * count * size * size
    pair = [(0, 1), (1, 0)]
    runs = runs_of(order)
    dma = pltpu.SemaphoreType.DMA

    sent = call(
        functools.partial(send_kernel, runs),
        [message],
        2 * unit,
        activations,
        cotangent,
        lu,
        rd,
        vmem=WHOLE_VMEM,
        scratch=[pltpu.VMEM(s, BF16) for s in (tall, tall, square, square, message)]
        + [dma((4,)), dma((2,))],
        in_specs=[IN_HBM] * 4,
        out_specs=IN_HBM,
    )
    first = exchange(sent, order)
    sent, hidden, pre_back = call(
        functools.partial(middle_kernel, runs, runs),
        [message, wide, wide],
        4 * unit,
        first,
        ru,
        ld,
        scratch=[pltpu.VMEM(message, BF16), dma((2,))],
        out_specs=[IN_HBM, IN_VMEM, IN_VMEM],
    )
    second = exchange(sent, order)
    mid = call(
        functools.partial(middle_grads_kernel, runs),
        [(2, *square)],
        2 * unit,
        first,
        hidden,
        pre_back,
    )
    mid_other = lax.ppermute(mid, "dp", pair)
    last = call(
        functools.partial(last_grads_kernel, runs),
        [(2, *square)],
        2 * unit,
        second,
        activations,
        cotangent,
    )
    last_other = lax.ppermute(last, "dp", pair)
    output, input_grad = call(
        functools.partial(last_kernel, runs), [tall, tall], 2 * unit, second, lu, rd
    )
    mid_sum = mid.astype(F32) + mid_other.astype(F32)
    last_sum = last.astype(F32) + last_other.astype(F32)
    return (output, input_grad, last_sum[1:], mid_sum[:1], mid_sum[1:], last_sum[:1])


def group_order():
    members = np.arange(math.prod(MP_AXES)).reshape(MP_AXES)
    far = [extent // 2 for extent in MP_AXES[:3]]
    return tuple(int(m) for m in np.roll(members, [-f for f in far], (0, 1, 2)).reshape(-1))


def solution(mesh):
    tokens, factor = P("dp", "mp"), P("mp", None, None)
    order = group_order()
    return jax.shard_map(
        functools.partial(body, order),
        mesh=mesh,
        in_specs=(tokens, factor, factor, factor, factor, tokens),
        out_specs=(tokens, tokens, factor, factor, factor, factor),
        check_vma=False,
    )
```

```python
import functools
import math

import jax
import jax.numpy as jnp
import numpy as np
from jax import lax
from jax.experimental import pallas as pl
from jax.experimental.pallas import tpu as pltpu
from jax.sharding import PartitionSpec as P

F32 = jnp.float32
BF16 = jnp.bfloat16
LANES = 128
MP_AXES = (4, 2, 8, 2)
IN_HBM = pl.BlockSpec(memory_space=pltpu.HBM)
IN_VMEM = pl.BlockSpec(memory_space=pltpu.VMEM)


def gelu_exact(value):
    return 0.5 * value * (1.0 + lax.erf(value / math.sqrt(2.0)))


def gelu_slope(value):
    cumul = 0.5 * (1.0 + lax.erf(value / math.sqrt(2.0)))
    density = jnp.exp(-0.5 * value * value) / math.sqrt(2.0 * math.pi)
    return cumul + value * density


def dot(a, b, ca, cb):
    return lax.dot_general(a, b, (((ca,), (cb,)), ((), ())), preferred_element_type=F32)


def runs_of(order):
    runs = []
    for position, member in enumerate(order):
        if runs and member == runs[-1][1] + runs[-1][2]:
            runs[-1][2] += 1
        else:
            runs.append([position, member, 1])
    return sorted((tuple(run) for run in runs), key=lambda run: run[1])


def put(ref, half, runs, flat):
    rows = ref.shape[1] // 2
    pieces = flat.astype(BF16).reshape(flat.shape[0], rows, LANES)
    for position, member, length in runs:
        ref[pl.ds(position, length), pl.ds(half * rows, rows), :] = pieces[member : member + length]


def take(ref, half, runs):
    rows = ref.shape[1] // 2
    pieces = [ref[pl.ds(p, length), pl.ds(half * rows, rows), :] for p, _, length in runs]
    pieces = pieces[0] if len(pieces) == 1 else jnp.concatenate(pieces, axis=0)
    return pieces.reshape(pieces.shape[0], rows * LANES)


def ship(half, out_ref, out_hbm, sems):
    rows = out_ref.shape[1] // 2
    part = pl.ds(half * rows, rows)
    return pltpu.make_async_copy(out_ref.at[:, part, :], out_hbm.at[:, part, :], sems.at[half])


def send_kernel(runs, x_hbm, g_hbm, lu_hbm, rd_hbm, out_ref, x_ref, g_ref, lu_ref, rd_ref, sems):
    pairs = ((lu_hbm, lu_ref), (x_hbm, x_ref), (rd_hbm, rd_ref), (g_hbm, g_ref))
    copies = [pltpu.make_async_copy(a, b, sems.at[i]) for i, (a, b) in enumerate(pairs)]
    for copy in copies:
        copy.start()
    copies[0].wait()
    copies[1].wait()
    put(out_ref, 0, runs, dot(lu_ref[...], x_ref[...], 0, 1))
    copies[2].wait()
    copies[3].wait()
    put(out_ref, 1, runs, dot(rd_ref[...], g_ref[...], 1, 1))


def middle_kernel(came, runs, recv_ref, ru_ref, ld_ref, out_hbm, hid_ref, pre_ref, out_ref, sems):
    ru, ld = ru_ref[...], ld_ref[...]
    pre_act = dot(ru, take(recv_ref, 0, came), 0, 0)
    hidden = gelu_exact(pre_act).astype(BF16)
    put(out_ref, 0, runs, dot(ld, hidden, 0, 0))
    first = ship(0, out_ref, out_hbm, sems)
    first.start()
    hid_ref[...] = hidden
    hidden_back = dot(ld, take(recv_ref, 1, came), 1, 0)
    pre_back = (hidden_back * gelu_slope(pre_act)).astype(BF16)
    put(out_ref, 1, runs, dot(ru, pre_back, 1, 0))
    second = ship(1, out_ref, out_hbm, sems)
    second.start()
    pre_ref[...] = pre_back
    first.wait()
    second.wait()


def middle_grads_kernel(came, recv_ref, hid_ref, pre_ref, grads_ref):
    grads_ref[0] = dot(take(recv_ref, 0, came), pre_ref[...], 1, 1).astype(BF16)
    grads_ref[1] = dot(hid_ref[...], take(recv_ref, 1, came), 1, 1).astype(BF16)


def last_grads_kernel(came, recv_ref, x_ref, g_ref, grads_ref):
    grads_ref[0] = dot(take(recv_ref, 0, came), g_ref[...], 1, 0).astype(BF16)
    grads_ref[1] = dot(take(recv_ref, 1, came), x_ref[...], 1, 0).T.astype(BF16)


def last_kernel(came, recv_ref, lu_ref, rd_ref, out_ref, back_ref):
    out_ref[...] = dot(take(recv_ref, 0, came), rd_ref[...], 0, 0).astype(BF16)
    back_ref[...] = dot(take(recv_ref, 1, came), lu_ref[...], 0, 1).astype(BF16)


def call(kernel, outs, flops, *args, scratch=(), **specs):
    moved = sum(a.size * 2 for a in args) + sum(math.prod(o) * 2 for o in outs)
    single = len(outs) == 1
    shapes = [jax.ShapeDtypeStruct(o, BF16) for o in outs]
    return pl.pallas_call(
        kernel,
        out_shape=shapes[0] if single else shapes,
        scratch_shapes=list(scratch),
        compiler_params=pltpu.CompilerParams(vmem_limit_bytes=48 * 1024 * 1024),
        cost_estimate=pl.CostEstimate(flops=flops, bytes_accessed=moved, transcendentals=0),
        **specs,
    )(*args)


def exchange(pieces, order):
    return lax.all_to_all(
        pieces, "mp", split_axis=0, concat_axis=0, tiled=True, axis_index_groups=[list(order)]
    )


def body(order, activations, left_up, right_up, left_down, right_down, cotangent):
    count, size = activations.shape
    lu, ru, ld, rd = (w.reshape(w.shape[1:]) for w in (left_up, right_up, left_down, right_down))
    message = (size, 2 * count // LANES, LANES)
    square, wide, tall = (size, size), (size, count), (count, size)
    unit = 2 * count * size * size
    pair = [(0, 1), (1, 0)]
    runs = runs_of(order)
    dma = pltpu.SemaphoreType.DMA

    sent = call(
        functools.partial(send_kernel, runs),
        [message],
        2 * unit,
        *(pltpu.with_memory_space_constraint(a, pltpu.HBM) for a in (activations, cotangent, lu, rd)),
        scratch=[pltpu.VMEM(s, BF16) for s in (tall, tall, square, square)] + [dma((4,))],
        in_specs=[IN_HBM] * 4,
    )
    first = exchange(sent, order)
    sent, hidden, pre_back = call(
        functools.partial(middle_kernel, runs, runs),
        [message, wide, wide],
        4 * unit,
        first,
        ru,
        ld,
        scratch=[pltpu.VMEM(message, BF16), dma((2,))],
        out_specs=[IN_HBM, IN_VMEM, IN_VMEM],
    )
    second = exchange(sent, order)
    mid = call(
        functools.partial(middle_grads_kernel, runs),
        [(2, *square)],
        2 * unit,
        first,
        hidden,
        pre_back,
    )
    mid_other = lax.ppermute(mid, "dp", pair)
    last = call(
        functools.partial(last_grads_kernel, runs),
        [(2, *square)],
        2 * unit,
        second,
        activations,
        cotangent,
    )
    last_other = lax.ppermute(last, "dp", pair)
    output, input_grad = call(
        functools.partial(last_kernel, runs), [tall, tall], 2 * unit, second, lu, rd
    )
    mid_sum = mid.astype(F32) + mid_other.astype(F32)
    last_sum = last.astype(F32) + last_other.astype(F32)
    return (output, input_grad, last_sum[1:], mid_sum[:1], mid_sum[1:], last_sum[:1])


def group_order():
    coords = [np.unravel_index(m, MP_AXES) for m in range(math.prod(MP_AXES))]
    far = int(np.ravel_multi_index([extent // 2 for extent in MP_AXES], MP_AXES))

    def hops(member):
        y, x, z, core = (int(c) for c in coords[member])
        return (min(y, MP_AXES[0] - y) + x + min(z, MP_AXES[2] - z), core)

    return (far, *sorted((m for m in range(len(coords)) if m != far), key=hops))


def solution(mesh):
    tokens, factor = P("dp", "mp"), P("mp", None, None)
    order = group_order()
    return jax.shard_map(
        functools.partial(body, order),
        mesh=mesh,
        in_specs=(tokens, factor, factor, factor, factor, tokens),
        out_specs=(tokens, tokens, factor, factor, factor, factor),
        check_vma=False,
    )
```

```python
import functools
import math

import jax
import jax.numpy as jnp
import numpy as np
from jax import lax
from jax.experimental import pallas as pl
from jax.experimental.pallas import tpu as pltpu
from jax.sharding import PartitionSpec as P

F32 = jnp.float32
BF16 = jnp.bfloat16
LANES = 128
MP_AXES = (4, 2, 8, 2)
IN_HBM = pl.BlockSpec(memory_space=pltpu.HBM)
IN_VMEM = pl.BlockSpec(memory_space=pltpu.VMEM)


def gelu_exact(value):
    return 0.5 * value * (1.0 + lax.erf(value / math.sqrt(2.0)))


def gelu_slope(value):
    cumul = 0.5 * (1.0 + lax.erf(value / math.sqrt(2.0)))
    density = jnp.exp(-0.5 * value * value) / math.sqrt(2.0 * math.pi)
    return cumul + value * density


def dot(a, b, ca, cb):
    return lax.dot_general(a, b, (((ca,), (cb,)), ((), ())), preferred_element_type=F32)


def runs_of(order):
    runs = []
    for position, member in enumerate(order):
        if runs and member == runs[-1][1] + runs[-1][2]:
            runs[-1][2] += 1
        else:
            runs.append([position, member, 1])
    return sorted((tuple(run) for run in runs), key=lambda run: run[1])


def put(ref, half, runs, flat):
    rows = ref.shape[1] // 2
    pieces = flat.astype(BF16).reshape(flat.shape[0], rows, LANES)
    for position, member, length in runs:
        ref[pl.ds(position, length), pl.ds(half * rows, rows), :] = pieces[member : member + length]


def take(ref, half, runs):
    rows = ref.shape[1] // 2
    pieces = [ref[pl.ds(p, length), pl.ds(half * rows, rows), :] for p, _, length in runs]
    pieces = pieces[0] if len(pieces) == 1 else jnp.concatenate(pieces, axis=0)
    return pieces.reshape(pieces.shape[0], rows * LANES)


def send_kernel(runs, x_hbm, g_hbm, lu_hbm, rd_hbm, out_ref, x_ref, g_ref, lu_ref, rd_ref, sems):
    pairs = ((lu_hbm, lu_ref), (x_hbm, x_ref), (rd_hbm, rd_ref), (g_hbm, g_ref))
    copies = [pltpu.make_async_copy(a, b, sems.at[i]) for i, (a, b) in enumerate(pairs)]
    for copy in copies:
        copy.start()
    copies[0].wait()
    copies[1].wait()
    put(out_ref, 0, runs, dot(lu_ref[...], x_ref[...], 0, 1))
    copies[2].wait()
    copies[3].wait()
    put(out_ref, 1, runs, dot(rd_ref[...], g_ref[...], 1, 1))


def middle_kernel(came, runs, recv_ref, ru_ref, ld_ref, out_ref, hid_ref, pre_ref):
    ru, ld = ru_ref[...], ld_ref[...]
    pre_act = dot(ru, take(recv_ref, 0, came), 0, 0)
    hidden = gelu_exact(pre_act).astype(BF16)
    hid_ref[...] = hidden
    put(out_ref, 0, runs, dot(ld, hidden, 0, 0))
    hidden_back = dot(ld, take(recv_ref, 1, came), 1, 0)
    pre_back = (hidden_back * gelu_slope(pre_act)).astype(BF16)
    put(out_ref, 1, runs, dot(ru, pre_back, 1, 0))
    pre_ref[...] = pre_back


def middle_grads_kernel(came, recv_ref, hid_ref, pre_ref, grads_ref):
    grads_ref[0] = dot(take(recv_ref, 0, came), pre_ref[...], 1, 1).astype(BF16)
    grads_ref[1] = dot(hid_ref[...], take(recv_ref, 1, came), 1, 1).astype(BF16)


def last_grads_kernel(came, recv_ref, x_ref, g_ref, grads_ref):
    grads_ref[0] = dot(take(recv_ref, 0, came), g_ref[...], 1, 0).astype(BF16)
    grads_ref[1] = dot(take(recv_ref, 1, came), x_ref[...], 1, 0).T.astype(BF16)


def last_kernel(came, recv_ref, lu_ref, rd_ref, out_ref, back_ref):
    out_ref[...] = dot(take(recv_ref, 0, came), rd_ref[...], 0, 0).astype(BF16)
    back_ref[...] = dot(take(recv_ref, 1, came), lu_ref[...], 0, 1).astype(BF16)


def call(kernel, outs, flops, *args, scratch=(), **specs):
    moved = sum(a.size * 2 for a in args) + sum(math.prod(o) * 2 for o in outs)
    single = len(outs) == 1
    shapes = [jax.ShapeDtypeStruct(o, BF16) for o in outs]
    return pl.pallas_call(
        kernel,
        out_shape=shapes[0] if single else shapes,
        scratch_shapes=list(scratch),
        compiler_params=pltpu.CompilerParams(vmem_limit_bytes=48 * 1024 * 1024),
        cost_estimate=pl.CostEstimate(flops=flops, bytes_accessed=moved, transcendentals=0),
        **specs,
    )(*args)


def exchange(pieces, order):
    return lax.all_to_all(
        pieces, "mp", split_axis=0, concat_axis=0, tiled=True, axis_index_groups=[list(order)]
    )


def body(order, activations, left_up, right_up, left_down, right_down, cotangent):
    count, size = activations.shape
    lu, ru, ld, rd = (w.reshape(w.shape[1:]) for w in (left_up, right_up, left_down, right_down))
    message = (size, 2 * count // LANES, LANES)
    square, wide, tall = (size, size), (size, count), (count, size)
    unit = 2 * count * size * size
    pair = [(0, 1), (1, 0)]
    runs = runs_of(order)
    dma = pltpu.SemaphoreType.DMA

    sent = call(
        functools.partial(send_kernel, runs),
        [message],
        2 * unit,
        *(pltpu.with_memory_space_constraint(a, pltpu.HBM) for a in (activations, cotangent, lu, rd)),
        scratch=[pltpu.VMEM(s, BF16) for s in (tall, tall, square, square)] + [dma((4,))],
        in_specs=[IN_HBM] * 4,
    )
    first = exchange(sent, order)
    sent, hidden, pre_back = call(
        functools.partial(middle_kernel, runs, runs),
        [message, wide, wide],
        4 * unit,
        first,
        ru,
        ld,
    )
    second = exchange(sent, order)
    mid = call(
        functools.partial(middle_grads_kernel, runs),
        [(2, *square)],
        2 * unit,
        first,
        hidden,
        pre_back,
    )
    mid_other = lax.ppermute(mid, "dp", pair)
    last = call(
        functools.partial(last_grads_kernel, runs),
        [(2, *square)],
        2 * unit,
        second,
        activations,
        cotangent,
    )
    last_other = lax.ppermute(last, "dp", pair)
    output, input_grad = call(
        functools.partial(last_kernel, runs), [tall, tall], 2 * unit, second, lu, rd
    )
    mid_sum = mid.astype(F32) + mid_other.astype(F32)
    last_sum = last.astype(F32) + last_other.astype(F32)
    return (output, input_grad, last_sum[1:], mid_sum[:1], mid_sum[1:], last_sum[:1])


def group_order():
    coords = [np.unravel_index(m, MP_AXES) for m in range(math.prod(MP_AXES))]
    far = int(np.ravel_multi_index([extent // 2 for extent in MP_AXES], MP_AXES))

    def hops(member):
        y, x, z, core = (int(c) for c in coords[member])
        return (-core, min(y, MP_AXES[0] - y) + x + min(z, MP_AXES[2] - z))

    return (far, *sorted((m for m in range(len(coords)) if m != far), key=hops))


def solution(mesh):
    tokens, factor = P("dp", "mp"), P("mp", None, None)
    order = group_order()
    return jax.shard_map(
        functools.partial(body, order),
        mesh=mesh,
        in_specs=(tokens, factor, factor, factor, factor, tokens),
        out_specs=(tokens, tokens, factor, factor, factor, factor),
        check_vma=False,
    )
```

```python
import functools
import math

import jax
import jax.numpy as jnp
import numpy as np
from jax import lax
from jax.experimental import pallas as pl
from jax.experimental.pallas import tpu as pltpu
from jax.sharding import PartitionSpec as P

F32 = jnp.float32
BF16 = jnp.bfloat16
LANES = 128
MP_AXES = (4, 2, 8, 2)
IN_HBM = pl.BlockSpec(memory_space=pltpu.HBM)
IN_VMEM = pl.BlockSpec(memory_space=pltpu.VMEM)


def gelu_and_slope(value):
    cumul = 0.5 * (1.0 + lax.erf(value / math.sqrt(2.0)))
    density = jnp.exp(-0.5 * value * value) / math.sqrt(2.0 * math.pi)
    return value * cumul, cumul + value * density


def dot(a, b, ca, cb):
    return lax.dot_general(a, b, (((ca,), (cb,)), ((), ())), preferred_element_type=F32)


def runs_of(order):
    runs = []
    for position, member in enumerate(order):
        if runs and member == runs[-1][1] + runs[-1][2]:
            runs[-1][2] += 1
        else:
            runs.append([position, member, 1])
    return sorted((tuple(run) for run in runs), key=lambda run: run[1])


def put(ref, half, runs, flat):
    rows = ref.shape[1] // 2
    pieces = flat.astype(BF16).reshape(flat.shape[0], rows, LANES)
    for position, member, length in runs:
        ref[pl.ds(position, length), pl.ds(half * rows, rows), :] = pieces[member : member + length]


def take(ref, half, runs):
    rows = ref.shape[1] // 2
    pieces = [ref[pl.ds(p, length), pl.ds(half * rows, rows), :] for p, _, length in runs]
    pieces = pieces[0] if len(pieces) == 1 else jnp.concatenate(pieces, axis=0)
    return pieces.reshape(pieces.shape[0], rows * LANES)


def send_kernel(runs, x_hbm, g_hbm, lu_hbm, rd_hbm, out_ref, x_ref, g_ref, lu_ref, rd_ref, sems):
    pairs = ((lu_hbm, lu_ref), (x_hbm, x_ref), (rd_hbm, rd_ref), (g_hbm, g_ref))
    copies = [pltpu.make_async_copy(a, b, sems.at[i]) for i, (a, b) in enumerate(pairs)]
    for copy in copies:
        copy.start()
    copies[0].wait()
    copies[1].wait()
    put(out_ref, 0, runs, dot(lu_ref[...], x_ref[...], 0, 1))
    copies[2].wait()
    copies[3].wait()
    put(out_ref, 1, runs, dot(rd_ref[...], g_ref[...], 1, 1))


def middle_kernel(came, runs, recv_ref, ru_ref, ld_ref, out_ref, hid_ref, pre_ref):
    ru, ld = ru_ref[...], ld_ref[...]
    pre_act = dot(ru, take(recv_ref, 0, came), 0, 0)
    hidden, slope = gelu_and_slope(pre_act)
    hidden = hidden.astype(BF16)
    hid_ref[...] = hidden
    put(out_ref, 0, runs, dot(ld, hidden, 0, 0))
    hidden_back = dot(ld, take(recv_ref, 1, came), 1, 0)
    pre_back = (hidden_back * slope).astype(BF16)
    put(out_ref, 1, runs, dot(ru, pre_back, 1, 0))
    pre_ref[...] = pre_back


def middle_grads_kernel(came, recv_ref, hid_ref, pre_ref, grads_ref):
    grads_ref[0] = dot(take(recv_ref, 0, came), pre_ref[...], 1, 1).astype(BF16)
    grads_ref[1] = dot(hid_ref[...], take(recv_ref, 1, came), 1, 1).astype(BF16)


def last_grads_kernel(came, recv_ref, x_ref, g_ref, grads_ref):
    grads_ref[0] = dot(take(recv_ref, 0, came), g_ref[...], 1, 0).astype(BF16)
    grads_ref[1] = dot(take(recv_ref, 1, came), x_ref[...], 1, 0).T.astype(BF16)


def last_kernel(came, recv_ref, lu_ref, rd_ref, out_ref, back_ref):
    out_ref[...] = dot(take(recv_ref, 0, came), rd_ref[...], 0, 0).astype(BF16)
    back_ref[...] = dot(take(recv_ref, 1, came), lu_ref[...], 0, 1).astype(BF16)


def call(kernel, outs, flops, *args, scratch=(), **specs):
    moved = sum(a.size * 2 for a in args) + sum(math.prod(o) * 2 for o in outs)
    single = len(outs) == 1
    shapes = [jax.ShapeDtypeStruct(o, BF16) for o in outs]
    return pl.pallas_call(
        kernel,
        out_shape=shapes[0] if single else shapes,
        scratch_shapes=list(scratch),
        compiler_params=pltpu.CompilerParams(vmem_limit_bytes=48 * 1024 * 1024),
        cost_estimate=pl.CostEstimate(flops=flops, bytes_accessed=moved, transcendentals=0),
        **specs,
    )(*args)


def exchange(pieces, order):
    return lax.all_to_all(
        pieces, "mp", split_axis=0, concat_axis=0, tiled=True, axis_index_groups=[list(order)]
    )


def body(order, activations, left_up, right_up, left_down, right_down, cotangent):
    count, size = activations.shape
    lu, ru, ld, rd = (w.reshape(w.shape[1:]) for w in (left_up, right_up, left_down, right_down))
    message = (size, 2 * count // LANES, LANES)
    square, wide, tall = (size, size), (size, count), (count, size)
    unit = 2 * count * size * size
    pair = [(0, 1), (1, 0)]
    runs = runs_of(order)
    dma = pltpu.SemaphoreType.DMA

    sent = call(
        functools.partial(send_kernel, runs),
        [message],
        2 * unit,
        *(pltpu.with_memory_space_constraint(a, pltpu.HBM) for a in (activations, cotangent, lu, rd)),
        scratch=[pltpu.VMEM(s, BF16) for s in (tall, tall, square, square)] + [dma((4,))],
        in_specs=[IN_HBM] * 4,
    )
    first = exchange(sent, order)
    sent, hidden, pre_back = call(
        functools.partial(middle_kernel, runs, runs),
        [message, wide, wide],
        4 * unit,
        first,
        ru,
        ld,
    )
    second = exchange(sent, order)
    mid = call(
        functools.partial(middle_grads_kernel, runs),
        [(2, *square)],
        2 * unit,
        first,
        hidden,
        pre_back,
    )
    mid_other = lax.ppermute(mid, "dp", pair)
    last = call(
        functools.partial(last_grads_kernel, runs),
        [(2, *square)],
        2 * unit,
        second,
        activations,
        cotangent,
    )
    last_other = lax.ppermute(last, "dp", pair)
    output, input_grad = call(
        functools.partial(last_kernel, runs), [tall, tall], 2 * unit, second, lu, rd
    )
    mid_sum = mid.astype(F32) + mid_other.astype(F32)
    last_sum = last.astype(F32) + last_other.astype(F32)
    return (output, input_grad, last_sum[1:], mid_sum[:1], mid_sum[1:], last_sum[:1])


def group_order():
    coords = [np.unravel_index(m, MP_AXES) for m in range(math.prod(MP_AXES))]
    far = int(np.ravel_multi_index([extent // 2 for extent in MP_AXES], MP_AXES))

    def hops(member):
        y, x, z, core = (int(c) for c in coords[member])
        up = min(y, MP_AXES[0] - y)
        return (-core, up, up + x + min(z, MP_AXES[2] - z))

    return (far, *sorted((m for m in range(len(coords)) if m != far), key=hops))


def solution(mesh):
    tokens, factor = P("dp", "mp"), P("mp", None, None)
    order = group_order()
    return jax.shard_map(
        functools.partial(body, order),
        mesh=mesh,
        in_specs=(tokens, factor, factor, factor, factor, tokens),
        out_specs=(tokens, tokens, factor, factor, factor, factor),
        check_vma=False,
    )
```
